32 devices in a mesh: bx: 8 (over y, x, core), by: 4 (over z).
Axes of the slice: x: 2, y: 2, z: 4, core: 2. Of those that a mesh axis runs over, the one named last changes fastest.
Arguments:
- particle_values: float32 [3, 65536], P(None, ('bx', 'by')), may hold values from -6 to 6
- destination: int32 [65536, 1], P(('bx', 'by')), may hold values from 0 to 31; in each aligned block of 2048 rows (0 to 2047, 2048 to 4095, ...) at most 128 rows name the same one
- cell_index: int32 [65536], P(('bx', 'by')), may hold values from 0 to 16383
- weight_in: bfloat16 [3, 3, 64, 9], replicated, may hold values from -0.625 to 0.625
- weight_mid: bfloat16 [3, 3, 64, 192], replicated, may hold values from -0.15625 to 0.15625
- weight_out: bfloat16 [3, 3, 64, 192], replicated, may hold values from -0.15625 to 0.15625
Outputs:
- spectrum: bfloat16 [2, 64, 16, 64, 512], P(None, None, 'bx', None, 'by')
The draws below stay inside these ranges and needn't reach their ends.
Inputs may be any that keep to these rules, and one draw needn't show every extreme that they name: `destination`: among the 2048 rows of one device, no brick is named more than 128 times; some brick is named exactly 128 times.
All inputs are finite; a program needn't handle non-finite values.
Results may differ from the reference program's by a relative error of at most 0.0074.
Values may be sent and summed in bfloat16 or wider, within the bound.
A program may use at most 192 MiB of HBM per device.

```python
import math
import jax
import jax.numpy as jnp
import numpy as np
from jax import lax

C = 64
F_IN = 3
CELL_X = 8
CELL_Y = 128
P_DEV = 2048
CAP = 128
CELLS = 16384
TOTAL_P = 65536
NX = 64
NY = 512
NZ = 16
N_BY = 4
DEVICES = 32


def touch_ends(array, rng, low, largest):
    longest = array.shape.index(max(array.shape))
    spots = []
    for shift in (0, 1):
        where = [jax.random.randint(jax.random.fold_in(rng, axis), (), 0, length) for axis, length in enumerate(array.shape)]
        where[longest] = (where[longest] + shift) % array.shape[longest]
        spots.append(tuple(where))
    return array.at[spots[0]].set(low).at[spots[1]].set(largest)


def levels(own_key, extent, cuts, smallest, top_value):
    level, own = 1.0, jax.random.fold_in(own_key, 6)
    for dim, shards_of in cuts:
        heights = jnp.exp(jax.random.uniform(jax.random.fold_in(own, dim), (shards_of,), jnp.float32, smallest / len(cuts), top_value / len(cuts)))
        level = level * jnp.repeat(heights, extent[dim] // shards_of).reshape([-1 if axis == dim else 1 for axis in range(len(extent))])
    return level


def deal_out(own_key, own, number, rows, count, top, most, slope):
    ranking = jax.random.permutation(own_key, count)
    heavy_load, ordinary = portions_of(count, rows * top, most, slope, True), portions_of(count, rows * top, most, slope, False)
    places = jnp.arange(count)

    def named(lengths, offset_by):
        used = int((lengths > 0).sum())
        fixed = max(1, used // 4)
        passed = fixed + (places - fixed + offset_by * (used - fixed)) % max(1, count - fixed)
        return jnp.zeros((count,), jnp.int32).at[ranking[jnp.where(places < fixed, places, passed)]].set(jnp.asarray(lengths, jnp.int32))

    lengths = jnp.where(number % 4 == 0, named(heavy_load, number // 4), named(ordinary, number - number // 4 - 1))
    mixed = jax.random.permutation(jax.random.fold_in(own, 3), count)
    giver, taker = mixed[0:count // 2 * 2:2], mixed[1:count // 2 * 2:2]
    margin = jnp.minimum(lengths[giver] - 1, most - lengths[taker]) // 2
    margin = jnp.where((giver == ranking[0]) | (taker == ranking[0]) | (lengths[taker] == 0), 0, jnp.maximum(margin, 0))
    passed = jax.random.randint(jax.random.fold_in(own, 4), (count // 2,), 0, 1 << 20) % (margin + 1)
    lengths = lengths.at[giver].add(-passed).at[taker].add(passed)
    members = jnp.searchsorted(jnp.cumsum(lengths), jnp.arange(rows * top), side="right").astype(jnp.int32)
    grid = members.reshape(top, rows).T
    grid = grid[jax.random.permutation(jax.random.fold_in(own, 1), rows)]
    offset_by = jax.random.randint(jax.random.fold_in(own, 2), (rows, 1), 0, top)
    return jnp.take_along_axis(grid, (jnp.arange(top)[None, :] + offset_by) % top, axis=1)


def portions_of(number_of, total, limit, slope, full):
    weights = [(1 << 20) // math.isqrt(rank ** slope) + 1 for rank in range(1, number_of + 1)]
    largest = limit if full else min(limit, max(-(-total // number_of), total * weights[0] // sum(weights)))
    least = 1 if total - largest >= number_of - 1 else 0
    given, rest = [largest] + [least] * (number_of - 1), total - largest - least * (number_of - 1)
    while rest > 0:
        movable = [i for i in range(1, number_of) if given[i] < largest] or [i for i in range(1, number_of) if given[i] < limit]
        pool, remaining = sum([weights[i] for i in movable]), rest
        for i in movable:
            extra = min(limit - given[i], max(1, remaining * weights[i] // pool), rest)
            given[i] = given[i] + extra
            rest = rest - extra
    return np.array(given)


def centred(rng, dims, scale, most, split=(), kind=jnp.bfloat16):
    factor_of = levels(rng, dims, split, -0.22, 0.18) if split else 1.0
    drawn = jax.random.normal(rng, dims, jnp.float32) * scale * factor_of
    return jnp.minimum(jnp.maximum(drawn, -most), most).astype(kind)


def setup_inputs(seed: int = 0) -> dict:
    key_of = jax.random.split(jax.random.key(seed), 7)
    particle_values = centred(key_of[0], (F_IN, TOTAL_P), 1.0, 6.0, ((1, 32),), jnp.float32)
    destination_keys = jax.random.split(jax.random.fold_in(key_of[1], 1), TOTAL_P // P_DEV)
    destination_turns = jax.random.permutation(jax.random.fold_in(key_of[1], 3), TOTAL_P // P_DEV)
    destination = jax.vmap(lambda own, number: deal_out(jax.random.fold_in(key_of[1], 2), own, number, P_DEV, DEVICES, 1, CAP, 2))(destination_keys, destination_turns).reshape((TOTAL_P, 1))
    cell_index = touch_ends(jax.random.randint(key_of[2], (TOTAL_P,), 0, CELLS), jax.random.fold_in(key_of[2], 1), 0, CELLS - 1).astype(jnp.int32)
    weight_in = centred(key_of[3], (3, 3, C, 3 * F_IN), (27 * F_IN) ** -0.5, 0.625)
    weight_mid = centred(key_of[4], (3, 3, C, 3 * C), (27 * C) ** -0.5, 0.15625)
    weight_out = centred(key_of[5], (3, 3, C, 3 * C), (27 * C) ** -0.5, 0.15625)
    return {"particle_values": particle_values, "destination": destination, "cell_index": cell_index, "weight_in": weight_in, "weight_mid": weight_mid, "weight_out": weight_out}


def convolve(field, weight, spacing):
    channels = field.shape[0]
    depth = field.shape[1]

    def one_plane(plane_z):
        summed = jnp.zeros((weight.shape[2], NX * NY), jnp.float32)
        for step_z in range(3):
            source_z = ((plane_z + (step_z - 1) * spacing) % depth).astype(jnp.int32)
            plane = lax.dynamic_index_in_dim(field, source_z, axis=1, keepdims=False)
            for step_x in range(3):
                for step_y in range(3):
                    shifted = jnp.roll(plane, (-(step_x - 1) * spacing, -(step_y - 1) * spacing), axis=(1, 2))
                    matrix = weight[step_x, step_y][:, step_z * channels:(step_z + 1) * channels]
                    summed = summed + jnp.dot(matrix, shifted.reshape(channels, NX * NY), preferred_element_type=jnp.float32)
        summed = summed.reshape(weight.shape[2], NX, NY)
        return jnp.where(summed > 0, summed, 0.1 * summed).astype(jnp.bfloat16)
    planes = lax.map(one_plane, jnp.arange(depth, dtype=jnp.int32))
    return jnp.transpose(planes, (1, 0, 2, 3))

def twiddle_table(count):
    position = jnp.arange(count, dtype=jnp.int32)
    phase = position[:, None] * position[None, :] % count
    angle = phase.astype(jnp.float32) * (2.0 * math.pi / count)
    factor = 1.0 / math.sqrt(count)
    return jnp.stack([jnp.cos(angle) * factor, -jnp.sin(angle) * factor]).astype(jnp.bfloat16)

def reference(particle_values, destination, cell_index, weight_in, weight_mid, weight_out):
    target = destination[:, 0]
    brick_x = target // N_BY
    brick_y = target % N_BY
    plane = cell_index // (CELL_X * CELL_Y)
    local_x = cell_index // CELL_Y % CELL_X
    local_y = cell_index % CELL_Y
    flat = (plane * NX + brick_x * CELL_X + local_x) * NY + brick_y * CELL_Y + local_y
    painted = jnp.zeros((F_IN, NZ * NX * NY), jnp.float32).at[:, flat].add(particle_values)
    painted = painted.reshape(F_IN, NZ, NX, NY).astype(jnp.bfloat16)
    first = convolve(painted, weight_in, 1)
    second = convolve(first, weight_mid, 2)
    third = convolve(second, weight_out, 1)
    twiddle = twiddle_table(NX).astype(jnp.float32)

    def per_channel(channel_field):
        result = jnp.einsum('tkx,zxy->tzky', twiddle, channel_field.astype(jnp.float32))
        return result.astype(jnp.bfloat16)
    spectrum = lax.map(per_channel, third)
    return jnp.transpose(spectrum, (1, 0, 2, 3, 4))
```

```python
import functools
import math

import jax
import jax.numpy as jnp
import numpy as np
from jax import lax
from jax.experimental import pallas as pl
from jax.experimental.pallas import tpu as pltpu
from jax.sharding import PartitionSpec as P

CELL_X = 8
CELL_Y = 128
CELL_Z = 16
CHANNELS = 64
COMPS = 3
HALO = 4
ROW = CELL_Y + 2 * HALO
NT = (((1,), (1,)), ((), ()))


def twiddle_table(count):
    position = jnp.arange(count, dtype=jnp.int32)
    phase = position[:, None] * position[None, :] % count
    angle = phase.astype(jnp.float32) * (2.0 * math.pi / count)
    factor = 1.0 / math.sqrt(count)
    return jnp.stack([jnp.cos(angle) * factor, -jnp.sin(angle) * factor]).astype(jnp.bfloat16)


def three_parts(value):
    high = value.astype(jnp.bfloat16).astype(jnp.float32)
    rest = value - high
    middle = rest.astype(jnp.bfloat16).astype(jnp.float32)
    return high, middle, rest - middle


def pack_kernel(dest_ref, cell_ref, value_ref, out_ref):
    bricks, _, capacity = out_ref.shape
    rows = dest_ref.shape[1]
    block = min(256, rows)
    upper = (
        lax.broadcasted_iota(jnp.int32, (block, block), 0)
        < lax.broadcasted_iota(jnp.int32, (block, block), 1)
    ).astype(jnp.float32).astype(jnp.bfloat16)
    brick_ids = lax.broadcasted_iota(jnp.int32, (bricks, block), 0)
    slot_ids = lax.broadcasted_iota(jnp.int32, (capacity, block), 0)
    start = jnp.zeros((bricks, 1), jnp.float32)
    total = jnp.zeros((12 * bricks, capacity), jnp.float32)
    for number in range(rows // block):
        span = slice(number * block, (number + 1) * block)
        hot = (brick_ids == dest_ref[:, span]).astype(jnp.float32)
        before = jnp.dot(hot.astype(jnp.bfloat16), upper, preferred_element_type=jnp.float32)
        slot = jnp.sum(hot * (before + start), axis=0, keepdims=True).astype(jnp.int32)
        start = start + jnp.sum(hot, axis=1, keepdims=True)
        slot_hot = (slot_ids == slot).astype(jnp.float32).astype(jnp.bfloat16)
        data = [cell_ref[:, span].astype(jnp.float32)]
        data += [value_ref[f : f + 1, span] for f in range(COMPS)]
        spread = [hot * part for row in data for part in three_parts(row)]
        total = total + lax.dot_general(
            jnp.concatenate(spread, axis=0).astype(jnp.bfloat16),
            slot_hot,
            NT,
            preferred_element_type=jnp.float32,
        )
    for w in range(COMPS + 1):
        parts = [total[(3 * w + i) * bricks : (3 * w + i + 1) * bricks] for i in range(3)]
        out_ref[:, w, :] = (parts[0] + parts[1]) + parts[2]


def pack(destination, cells, values, devices_all, capacity):
    return pl.pallas_call(
        pack_kernel,
        out_shape=jax.ShapeDtypeStruct((devices_all, COMPS + 1, capacity), jnp.float32),
        in_specs=[pl.BlockSpec(memory_space=pltpu.VMEM)] * 3,
        out_specs=pl.BlockSpec(memory_space=pltpu.VMEM),
        compiler_params=pltpu.CompilerParams(vmem_limit_bytes=48 * 2**20),
        name="pack",
    )(destination, cells, values)


def paint_kernel(cell_ref, value_ref, out_ref):
    rows = cell_ref.shape[1]
    block = min(512, rows)
    lines = CELL_Z * CELL_X
    high_ids = lax.broadcasted_iota(jnp.int32, (lines, block), 0)
    total = jnp.zeros((lines, 9 * CELL_Y), jnp.float32)
    for number in range(rows // block):
        span = slice(number * block, (number + 1) * block)
        cell = cell_ref[:, span].astype(jnp.int32)
        high_hot = (high_ids == cell // CELL_Y).astype(jnp.float32).astype(jnp.bfloat16)
        low_hot = (high_ids == cell % CELL_Y).astype(jnp.float32)
        spread = []
        for f in range(COMPS):
            for part in three_parts(value_ref[f : f + 1, span]):
                spread.append((low_hot * part).astype(jnp.bfloat16))
        total = total + lax.dot_general(
            high_hot, jnp.concatenate(spread, axis=0), NT, preferred_element_type=jnp.float32
        )
    for f in range(COMPS):
        parts = [total[:, (3 * f + i) * CELL_Y : (3 * f + i + 1) * CELL_Y] for i in range(3)]
        out_ref[:, f * CELL_Y : (f + 1) * CELL_Y] = (
            (parts[0] + parts[1]) + parts[2]
        ).astype(jnp.bfloat16)


def paint(cells, values):
    lines = CELL_Z * CELL_X
    return pl.pallas_call(
        paint_kernel,
        out_shape=jax.ShapeDtypeStruct((lines, COMPS * CELL_Y), jnp.bfloat16),
        in_specs=[pl.BlockSpec(memory_space=pltpu.VMEM)] * 2,
        out_specs=pl.BlockSpec(memory_space=pltpu.VMEM),
        compiler_params=pltpu.CompilerParams(vmem_limit_bytes=48 * 2**20),
        name="paint",
    )(cells, values)


def up(number):
    return -(-number // 128) * 128


WIDE_0 = up((CELL_X + 8) * ROW)
WIDE_1 = up((CELL_X + 6) * ROW)
WIDE_2 = up((CELL_X + 2) * ROW)
WIDE_3 = up(CELL_X * ROW)
HELD_0 = WIDE_0 + 128
HELD_1 = WIDE_1 + 128
HELD_2 = WIDE_2 + 128
TAPS_1 = 512


def chunks(width):
    return [(at, min(256, width - at)) for at in range(0, width, 256)]


def window(load, offset, size):
    first, turn = offset // 128 * 128, offset % 128
    if turn == 0:
        return load(first, size)
    return pltpu.roll(load(first, size + 128), size + 128 - turn, 1)[:, :size]


def leaky(value):
    return jnp.maximum(value, 0.1 * value)


def conv_kernel(painted_ref, pick_ref, w1_ref, w2_ref, w3_ref, out_ref, big, first, second, total):
    depth = CELL_Z

    def spread_weight(z, carry):
        rows = pl.ds(pl.multiple_of(z * CHANNELS, CHANNELS), CHANNELS)
        big[rows, :] = jnp.dot(
            w1_ref[...], pick_ref[z], preferred_element_type=jnp.float32
        ).astype(jnp.bfloat16)
        return carry

    lax.fori_loop(0, depth, spread_weight, 0)
    planes = painted_ref.shape[0]
    for z in range(depth):
        first[z, :, WIDE_1:] = jnp.zeros((CHANNELS, HELD_1 - WIDE_1), jnp.bfloat16)
        second[z, :, WIDE_2:] = jnp.zeros((CHANNELS, HELD_2 - WIDE_2), jnp.bfloat16)
    for at, size in chunks(WIDE_1):
        pieces = [
            window(lambda a, n: painted_ref[:, a : a + n], at + tx * ROW + ty, size)
            for tx in range(3)
            for ty in range(3)
        ]
        pieces.append(jnp.zeros((TAPS_1 - 9 * planes, size), jnp.bfloat16))
        taps = jnp.concatenate(pieces, axis=0)

        def four(g, carry):
            rows = pl.ds(pl.multiple_of(g * 4 * CHANNELS, 4 * CHANNELS), 4 * CHANNELS)
            value = leaky(jnp.dot(big[rows, :], taps, preferred_element_type=jnp.float32))
            value = value.astype(jnp.bfloat16)
            for i in range(4):
                first[g * 4 + i, :, at : at + size] = value[i * CHANNELS : (i + 1) * CHANNELS]
            return carry

        for g in range(depth // 4):
            four(g, 0)

    def layer(source, weight_ref, spacing, width):
        def clear(z, carry):
            total[z, :, :width] = jnp.zeros((CHANNELS, width), jnp.float32)
            return carry

        lax.fori_loop(0, depth, clear, 0)

        def plane(z, carry):
            for at, size in chunks(width):
                taps = jnp.concatenate(
                    [
                        window(
                            lambda a, n: source[z, :, a : a + n],
                            at + (tx * ROW + ty) * spacing,
                            size,
                        )
                        for tx in range(3)
                        for ty in range(3)
                    ],
                    axis=0,
                )
                value = jnp.dot(weight_ref[...], taps, preferred_element_type=jnp.float32)
                for tz in range(3):
                    to = lax.rem(z - (tz - 1) * spacing + depth, depth)
                    total[to, :, at : at + size] += value[tz * CHANNELS : (tz + 1) * CHANNELS]
            return carry

        lax.fori_loop(0, depth, plane, 0)

    layer(first, w2_ref, 2, WIDE_2)

    def finish_second(z, carry):
        second[z, :, :WIDE_2] = leaky(total[z]).astype(jnp.bfloat16)
        return carry

    lax.fori_loop(0, depth, finish_second, 0)
    layer(second, w3_ref, 1, WIDE_3)

    def finish_third(z, carry):
        value = leaky(total[z, :, :WIDE_3])
        for x in range(CELL_X):
            out_ref[z, x] = value[:, x * ROW : x * ROW + CELL_Y].astype(jnp.bfloat16)
        return carry

    lax.fori_loop(0, depth, finish_third, 0)


def pick_table():
    table = np.zeros((CELL_Z, 9, 3, COMPS, TAPS_1), np.float32)
    for z in range(CELL_Z):
        for tap in range(9):
            for tz in range(3):
                for i in range(COMPS):
                    plane = (z + tz - 1) % CELL_Z
                    table[z, tap, tz, i, tap * CELL_Z * COMPS + plane * COMPS + i] = 1
    return table.reshape(CELL_Z, 27 * COMPS, TAPS_1)


def convolve_all(painted, weight_in, weight_mid, weight_out):
    pick = jnp.asarray(pick_table(), jnp.bfloat16)
    w1 = jnp.transpose(weight_in, (2, 0, 1, 3)).reshape(CHANNELS, 27 * COMPS)

    def arranged(weight):
        split = weight.reshape(3, 3, CHANNELS, 3, CHANNELS)
        return jnp.transpose(split, (3, 2, 0, 1, 4)).reshape(3 * CHANNELS, 9 * CHANNELS)

    return pl.pallas_call(
        conv_kernel,
        out_shape=jax.ShapeDtypeStruct((CELL_Z, CELL_X, CHANNELS, CELL_Y), jnp.bfloat16),
        in_specs=[pl.BlockSpec(memory_space=pltpu.VMEM)] * 5,
        out_specs=pl.BlockSpec(memory_space=pltpu.VMEM),
        scratch_shapes=[
            pltpu.VMEM((CELL_Z * CHANNELS, TAPS_1), jnp.bfloat16),
            pltpu.VMEM((CELL_Z, CHANNELS, HELD_1), jnp.bfloat16),
            pltpu.VMEM((CELL_Z, CHANNELS, HELD_2), jnp.bfloat16),
            pltpu.VMEM((CELL_Z, CHANNELS, WIDE_2), jnp.float32),
        ],
        compiler_params=pltpu.CompilerParams(vmem_limit_bytes=48 * 2**20),
        name="convolutions",
    )(painted, pick, w1, arranged(weight_mid), arranged(weight_out))


def extended(cells, axis, dim):
    count = lax.axis_size(axis)
    size = cells.shape[dim]
    head = lax.slice_in_dim(cells, 0, HALO, axis=dim)
    tail = lax.slice_in_dim(cells, size - HALO, size, axis=dim)
    return jnp.concatenate(
        [
            lax.ppermute(tail, axis, [(i, (i + 1) % count) for i in range(count)]),
            cells,
            lax.ppermute(head, axis, [((i + 1) % count, i) for i in range(count)]),
        ],
        axis=dim,
    )


def on_device(particle_values, destination, cell_index, weight_in, weight_mid, weight_out):
    devices_all = lax.axis_size("bx") * lax.axis_size("by")
    rows_here = cell_index.shape[0]
    capacity = 2 * rows_here // devices_all
    outgoing = pack(
        destination.reshape(1, rows_here),
        cell_index.reshape(1, rows_here),
        particle_values,
        devices_all,
        capacity,
    )
    incoming = lax.all_to_all(outgoing, ("bx", "by"), split_axis=0, concat_axis=0, tiled=True)
    incoming = jnp.transpose(incoming, (1, 0, 2)).reshape(COMPS + 1, devices_all * capacity)
    painted = paint(incoming[:1], incoming[1:])
    cells = painted.reshape(CELL_Z, CELL_X, COMPS, CELL_Y)
    cells = extended(extended(cells, "bx", 1), "by", 3)
    cells = jnp.transpose(cells, (0, 2, 1, 3)).reshape(CELL_Z * COMPS, (CELL_X + 8) * ROW)
    cells = jnp.pad(cells, ((0, 0), (0, HELD_0 - cells.shape[1])))
    third = convolve_all(cells, weight_in, weight_mid, weight_out)
    moved = lax.all_to_all(third, "bx", split_axis=0, concat_axis=1, tiled=True)
    twiddle = twiddle_table(moved.shape[1])
    return jnp.einsum(
        "tkx,zxcy->tczky", twiddle, moved, preferred_element_type=jnp.float32
    ).astype(jnp.bfloat16)


def solution(mesh):
    placed = (P(None, ("bx", "by")), P(("bx", "by"), None), P(("bx", "by")), P(), P(), P())
    return jax.shard_map(
        on_device,
        mesh=mesh,
        in_specs=placed,
        out_specs=P(None, None, "bx", None, "by"),
        check_vma=False,
    )
```

```python
import functools
import math

import jax
import jax.numpy as jnp
import numpy as np
from jax import lax
from jax.experimental import pallas as pl
from jax.experimental.pallas import tpu as pltpu
from jax.sharding import PartitionSpec as P

CELL_X = 8
CELL_Y = 128
CELL_Z = 16
CHANNELS = 64
COMPS = 3
HALO = 4
ROW = CELL_Y + 2 * HALO
NT = (((1,), (1,)), ((), ()))


def twiddle_table(count):
    position = jnp.arange(count, dtype=jnp.int32)
    phase = position[:, None] * position[None, :] % count
    angle = phase.astype(jnp.float32) * (2.0 * math.pi / count)
    factor = 1.0 / math.sqrt(count)
    return jnp.stack([jnp.cos(angle) * factor, -jnp.sin(angle) * factor]).astype(jnp.bfloat16)


def three_parts(value):
    high = value.astype(jnp.bfloat16).astype(jnp.float32)
    rest = value - high
    middle = rest.astype(jnp.bfloat16).astype(jnp.float32)
    return high, middle, rest - middle


def pack_kernel(dest_ref, cell_ref, value_ref, out_ref):
    bricks, _, capacity = out_ref.shape
    rows = dest_ref.shape[1]
    block = min(256, rows)
    upper = (
        lax.broadcasted_iota(jnp.int32, (block, block), 0)
        < lax.broadcasted_iota(jnp.int32, (block, block), 1)
    ).astype(jnp.float32).astype(jnp.bfloat16)
    brick_ids = lax.broadcasted_iota(jnp.int32, (bricks, block), 0)
    slot_ids = lax.broadcasted_iota(jnp.int32, (capacity, block), 0)
    start = jnp.zeros((bricks, 1), jnp.float32)
    total = jnp.zeros((12 * bricks, capacity), jnp.float32)
    for number in range(rows // block):
        span = slice(number * block, (number + 1) * block)
        hot = (brick_ids == dest_ref[:, span]).astype(jnp.float32)
        before = jnp.dot(hot.astype(jnp.bfloat16), upper, preferred_element_type=jnp.float32)
        slot = jnp.sum(hot * (before + start), axis=0, keepdims=True).astype(jnp.int32)
        start = start + jnp.sum(hot, axis=1, keepdims=True)
        slot_hot = (slot_ids == slot).astype(jnp.float32).astype(jnp.bfloat16)
        data = [cell_ref[:, span].astype(jnp.float32)]
        data += [value_ref[f : f + 1, span] for f in range(COMPS)]
        spread = [hot * part for row in data for part in three_parts(row)]
        total = total + lax.dot_general(
            jnp.concatenate(spread, axis=0).astype(jnp.bfloat16),
            slot_hot,
            NT,
            preferred_element_type=jnp.float32,
        )
    for w in range(COMPS + 1):
        parts = [total[(3 * w + i) * bricks : (3 * w + i + 1) * bricks] for i in range(3)]
        out_ref[:, w, :] = (parts[0] + parts[1]) + parts[2]


def pack(destination, cells, values, devices_all, capacity):
    return pl.pallas_call(
        pack_kernel,
        out_shape=jax.ShapeDtypeStruct((devices_all, COMPS + 1, capacity), jnp.float32),
        in_specs=[pl.BlockSpec(memory_space=pltpu.VMEM)] * 3,
        out_specs=pl.BlockSpec(memory_space=pltpu.VMEM),
        compiler_params=pltpu.CompilerParams(vmem_limit_bytes=48 * 2**20),
        name="pack",
    )(destination, cells, values)


def paint_kernel(cell_ref, value_ref, out_ref):
    rows = cell_ref.shape[1]
    block = min(512, rows)
    lines = CELL_Z * CELL_X
    high_ids = lax.broadcasted_iota(jnp.int32, (lines, block), 0)
    total = jnp.zeros((lines, 9 * CELL_Y), jnp.float32)
    for number in range(rows // block):
        span = slice(number * block, (number + 1) * block)
        cell = cell_ref[:, span].astype(jnp.int32)
        high_hot = (high_ids == cell // CELL_Y).astype(jnp.float32).astype(jnp.bfloat16)
        low_hot = (high_ids == cell % CELL_Y).astype(jnp.float32)
        spread = []
        for f in range(COMPS):
            for part in three_parts(value_ref[f : f + 1, span]):
                spread.append((low_hot * part).astype(jnp.bfloat16))
        total = total + lax.dot_general(
            high_hot, jnp.concatenate(spread, axis=0), NT, preferred_element_type=jnp.float32
        )
    for f in range(COMPS):
        parts = [total[:, (3 * f + i) * CELL_Y : (3 * f + i + 1) * CELL_Y] for i in range(3)]
        out_ref[:, f * CELL_Y : (f + 1) * CELL_Y] = (
            (parts[0] + parts[1]) + parts[2]
        ).astype(jnp.bfloat16)


def paint(cells, values):
    lines = CELL_Z * CELL_X
    return pl.pallas_call(
        paint_kernel,
        out_shape=jax.ShapeDtypeStruct((lines, COMPS * CELL_Y), jnp.bfloat16),
        in_specs=[pl.BlockSpec(memory_space=pltpu.VMEM)] * 2,
        out_specs=pl.BlockSpec(memory_space=pltpu.VMEM),
        compiler_params=pltpu.CompilerParams(vmem_limit_bytes=48 * 2**20),
        name="paint",
    )(cells, values)


def up(number):
    return -(-number // 128) * 128


WIDE_0 = up((CELL_X + 8) * ROW)
WIDE_1 = up((CELL_X + 6) * ROW)
WIDE_2 = up((CELL_X + 2) * ROW)
WIDE_3 = up(CELL_X * ROW)
HELD_0 = WIDE_0 + 128
HELD_1 = WIDE_1 + 128
HELD_2 = WIDE_2 + 128
TAPS_1 = 512


def chunks(width):
    return [(at, min(256, width - at)) for at in range(0, width, 256)]


def window(load, offset, size):
    first, turn = offset // 128 * 128, offset % 128
    if turn == 0:
        return load(first, size)
    return pltpu.roll(load(first, size + 128), size + 128 - turn, 1)[:, :size]


def leaky(value):
    return jnp.maximum(value, 0.1 * value)


MESH = pl.DeviceIdType.MESH
PLANES = CELL_Z * COMPS


def neighbours(count_x, count_y, me_x, me_y):
    around = []
    for dx in (-1, 0, 1):
        for dy in (-1, 0, 1):
            if dx or dy:
                place = (lax.rem(me_x + dx + count_x, count_x), lax.rem(me_y + dy + count_y, count_y))
                around.append((dx, dy, place))
    return around


def conv_kernel(
    count_x,
    count_y,
    cells_ref,
    edge_ref,
    pick_ref,
    w1_ref,
    w2_ref,
    w3_ref,
    out_ref,
    side,
    corner,
    painted,
    big,
    mid,
    last,
    first,
    second,
    total_2,
    total_3,
    third,
    halo_send,
    halo_recv,
    plane_send,
    plane_recv,
):
    depth = CELL_Z
    share = depth // count_x
    me_x, me_y = lax.axis_index("bx"), lax.axis_index("by")
    around = neighbours(count_x, count_y, me_x, me_y)

    barrier = pltpu.get_barrier_semaphore()
    for step in range(1, count_x):
        pl.semaphore_signal(
            barrier,
            inc=1,
            device_id=(lax.rem(me_x + step, count_x), me_y),
            device_id_type=MESH,
        )
    for dx, dy, place in around:
        if dy:
            pl.semaphore_signal(barrier, inc=1, device_id=place, device_id_type=MESH)
    pl.semaphore_wait(barrier, count_x - 1 + 6)

    halo = []
    for number, (dx, dy, place) in enumerate(around):
        if dy:
            slot = (1 - dx) * 2 + (0 if dy == 1 else 1)
            source, target = edge_ref, corner.at[slot]
        elif dx == 1:
            source, target = cells_ref.at[:, HALO * CELL_Y :], side.at[0]
        else:
            source, target = cells_ref.at[:, : HALO * CELL_Y], side.at[1]
        copy = pltpu.make_async_remote_copy(
            src_ref=source,
            dst_ref=target,
            send_sem=halo_send.at[number],
            recv_sem=halo_recv.at[number],
            device_id=place,
            device_id_type=MESH,
        )
        copy.start()
        halo.append(copy)

    def spread_weight(z, carry):
        rows = pl.ds(pl.multiple_of(z * CHANNELS, CHANNELS), CHANNELS)
        big[rows, :] = jnp.dot(
            w1_ref[...], pick_ref[z], preferred_element_type=jnp.float32
        ).astype(jnp.bfloat16)
        return carry

    lax.fori_loop(0, depth, spread_weight, 0)
    for source, target in ((w2_ref, mid), (w3_ref, last)):
        for tz in range(3):
            blocks = [
                source[tap // 3, tap % 3][:, tz * CHANNELS : (tz + 1) * CHANNELS]
                for tap in range(9)
            ]
            target[tz * CHANNELS : (tz + 1) * CHANNELS, :] = jnp.concatenate(blocks, axis=1)

    def clear(z, carry):
        total_2[z] = jnp.zeros((CHANNELS, WIDE_2), jnp.float32)
        total_3[z] = jnp.zeros((CHANNELS, WIDE_3), jnp.float32)
        first[z, :, WIDE_1:] = jnp.zeros((CHANNELS, HELD_1 - WIDE_1), jnp.bfloat16)
        second[z, :, WIDE_2:] = jnp.zeros((CHANNELS, HELD_2 - WIDE_2), jnp.bfloat16)
        return carry

    lax.fori_loop(0, depth, clear, 0)
    for copy in halo:
        copy.wait()

    lanes = lax.broadcasted_iota(jnp.int32, (PLANES, CELL_Y), 1)
    before = None
    for row in range(CELL_X + 2 * HALO):
        if row < HALO:
            centre, x, group = side[0, :, row * CELL_Y : (row + 1) * CELL_Y], row + HALO, 0
        elif row < HALO + CELL_X:
            x, group = row - HALO, 1
            centre = cells_ref[:, x * CELL_Y : (x + 1) * CELL_Y]
        else:
            x, group = row - HALO - CELL_X, 2
            centre = side[1, :, x * CELL_Y : (x + 1) * CELL_Y]
        under = pltpu.roll(corner[2 * group].astype(jnp.float32), 120 - 8 * x, 1)
        over = corner[2 * group + 1].astype(jnp.float32)
        if x:
            over = pltpu.roll(over, CELL_Y - 8 * x, 1)
        joined = jnp.concatenate(
            [centre.astype(jnp.float32), jnp.where(lanes < 64, over, under)], axis=1
        )
        joined = pltpu.roll(joined, 8 * row + HALO, 1)
        tile = joined[:, :CELL_Y]
        if row:
            tile = jnp.where(lanes < 8 * row, before, tile)
        painted[:, row * CELL_Y : (row + 1) * CELL_Y] = tile.astype(jnp.bfloat16)
        before = joined[:, CELL_Y:]
    painted[:, 16 * CELL_Y : 17 * CELL_Y] = before.astype(jnp.bfloat16)
    painted[:, WIDE_0:] = jnp.zeros((PLANES, HELD_0 - WIDE_0), jnp.bfloat16)

    for at, size in chunks(WIDE_1):
        pieces = [
            window(lambda a, n: painted[:, a : a + n], at + tx * ROW + ty, size)
            for tx in range(3)
            for ty in range(3)
        ]
        pieces.append(jnp.zeros((TAPS_1 - 9 * PLANES, size), jnp.bfloat16))
        taps = jnp.concatenate(pieces, axis=0)
        for g in range(depth // 4):
            rows = slice(g * 4 * CHANNELS, (g + 1) * 4 * CHANNELS)
            value = leaky(jnp.dot(big[rows, :], taps, preferred_element_type=jnp.float32))
            value = value.astype(jnp.bfloat16)
            for i in range(4):
                first[g * 4 + i, :, at : at + size] = value[i * CHANNELS : (i + 1) * CHANNELS]

    def add_plane(source, weight_ref, total, spacing, width, z):
        for at, size in chunks(width):
            taps = jnp.concatenate(
                [
                    window(
                        lambda a, n: source[z, :, a : a + n],
                        at + (tx * ROW + ty) * spacing,
                        size,
                    )
                    for tx in range(3)
                    for ty in range(3)
                ],
                axis=0,
            )
            value = jnp.dot(weight_ref[...], taps, preferred_element_type=jnp.float32)
            for tz in range(3):
                to = lax.rem(z - (tz - 1) * spacing + depth, depth)
                total[to, :, at : at + size] += value[tz * CHANNELS : (tz + 1) * CHANNELS]

    def plane_copy(z):
        owner = z // share
        return pltpu.make_async_remote_copy(
            src_ref=third.at[z],
            dst_ref=out_ref.at[lax.rem(z, share), pl.ds(me_x * CELL_X, CELL_X)],
            send_sem=plane_send.at[z],
            recv_sem=plane_recv.at[me_x * share + lax.rem(z, share)],
            device_id=(owner, me_y),
            device_id_type=MESH,
        )

    begin = (me_x + 1) * share - 3 + depth

    def turn(step, carry):
        @pl.when(step < depth)
        def _():
            add_plane(first, mid, total_2, 2, WIDE_2, lax.rem(begin + step, depth))

        @pl.when((step >= 4) & (step < depth + 4))
        def _():
            z = lax.rem(begin + step - 2, depth)
            second[z, :, :WIDE_2] = leaky(total_2[z]).astype(jnp.bfloat16)
            add_plane(second, last, total_3, 1, WIDE_3, z)

        @pl.when(step >= 6)
        def _():
            z = lax.rem(begin + step - 3, depth)
            value = leaky(total_3[z])
            for x in range(CELL_X):
                third[z, x] = value[:, x * ROW : x * ROW + CELL_Y].astype(jnp.bfloat16)

            @pl.when(z // share == me_x)
            def _():
                out_ref[lax.rem(z, share), pl.ds(me_x * CELL_X, CELL_X)] = third[z]

            @pl.when(z // share != me_x)
            def _():
                plane_copy(z).start()

        return carry

    lax.fori_loop(0, depth + 6, turn, 0)

    def settle(number, carry):
        other = number // share

        @pl.when(other != me_x)
        def _():
            plane_copy(number).wait_send()
            inner = lax.rem(number, share)
            pltpu.make_async_remote_copy(
                src_ref=third.at[number],
                dst_ref=out_ref.at[inner, pl.ds(other * CELL_X, CELL_X)],
                send_sem=plane_send.at[number],
                recv_sem=plane_recv.at[number],
                device_id=(other, me_y),
                device_id_type=MESH,
            ).wait_recv()

        return carry

    lax.fori_loop(0, depth, settle, 0)


def pick_table():
    table = np.zeros((CELL_Z, 9, 3, COMPS, TAPS_1), np.float32)
    for z in range(CELL_Z):
        for tap in range(9):
            for tz in range(3):
                for i in range(COMPS):
                    plane = (z + tz - 1) % CELL_Z
                    table[z, tap, tz, i, tap * CELL_Z * COMPS + plane * COMPS + i] = 1
    return table.reshape(CELL_Z, 27 * COMPS, TAPS_1)


def convolve_all(cells, edge, weight_in, weight_mid, weight_out):
    count_x, count_y = lax.axis_size("bx"), lax.axis_size("by")
    share = CELL_Z // count_x
    pick = jnp.asarray(pick_table(), jnp.bfloat16)
    w1 = jnp.transpose(weight_in, (2, 0, 1, 3)).reshape(CHANNELS, 27 * COMPS)
    half = jnp.bfloat16
    return pl.pallas_call(
        functools.partial(conv_kernel, count_x, count_y),
        out_shape=jax.ShapeDtypeStruct((share, count_x * CELL_X, CHANNELS, CELL_Y), half),
        in_specs=[pl.BlockSpec(memory_space=pltpu.VMEM)] * 6,
        out_specs=pl.BlockSpec(memory_space=pltpu.VMEM),
        scratch_shapes=[
            pltpu.VMEM((2, PLANES, HALO * CELL_Y), half),
            pltpu.VMEM((6, PLANES, CELL_Y), half),
            pltpu.VMEM((PLANES, HELD_0), half),
            pltpu.VMEM((CELL_Z * CHANNELS, TAPS_1), half),
            pltpu.VMEM((3 * CHANNELS, 9 * CHANNELS), half),
            pltpu.VMEM((3 * CHANNELS, 9 * CHANNELS), half),
            pltpu.VMEM((CELL_Z, CHANNELS, HELD_1), half),
            pltpu.VMEM((CELL_Z, CHANNELS, HELD_2), half),
            pltpu.VMEM((CELL_Z, CHANNELS, WIDE_2), jnp.float32),
            pltpu.VMEM((CELL_Z, CHANNELS, WIDE_3), jnp.float32),
            pltpu.VMEM((CELL_Z, CELL_X, CHANNELS, CELL_Y), half),
            pltpu.SemaphoreType.DMA((8,)),
            pltpu.SemaphoreType.DMA((8,)),
            pltpu.SemaphoreType.DMA((CELL_Z,)),
            pltpu.SemaphoreType.DMA((CELL_Z,)),
        ],
        compiler_params=pltpu.CompilerParams(
            vmem_limit_bytes=48 * 2**20, collective_id=0, has_side_effects=True
        ),
        name="convolutions",
    )(cells, edge, pick, w1, weight_mid, weight_out)


def on_device(particle_values, destination, cell_index, weight_in, weight_mid, weight_out):
    devices_all = lax.axis_size("bx") * lax.axis_size("by")
    rows_here = cell_index.shape[0]
    capacity = 2 * rows_here // devices_all
    outgoing = pack(
        destination.reshape(1, rows_here),
        cell_index.reshape(1, rows_here),
        particle_values,
        devices_all,
        capacity,
    )
    incoming = lax.all_to_all(outgoing, ("bx", "by"), split_axis=0, concat_axis=0, tiled=True)
    incoming = jnp.transpose(incoming, (1, 0, 2)).reshape(COMPS + 1, devices_all * capacity)
    painted = paint(incoming[:1], incoming[1:])
    cells = painted.reshape(CELL_Z, CELL_X, COMPS, CELL_Y)
    cells = jnp.transpose(cells, (0, 2, 1, 3))
    edge = jnp.concatenate([cells[..., :HALO], cells[..., CELL_Y - HALO :]], axis=3)
    edge = jnp.pad(edge.reshape(PLANES, 8 * CELL_X), ((0, 0), (0, CELL_Y - 8 * CELL_X)))
    cells = cells.reshape(PLANES, CELL_X * CELL_Y)
    moved = convolve_all(cells, edge, weight_in, weight_mid, weight_out)
    twiddle = twiddle_table(moved.shape[1])
    return jnp.einsum(
        "tkx,zxcy->tczky", twiddle, moved, preferred_element_type=jnp.float32
    ).astype(jnp.bfloat16)


def solution(mesh):
    placed = (P(None, ("bx", "by")), P(("bx", "by"), None), P(("bx", "by")), P(), P(), P())
    return jax.shard_map(
        on_device,
        mesh=mesh,
        in_specs=placed,
        out_specs=P(None, None, "bx", None, "by"),
        check_vma=False,
    )
```

```python
import functools
import math

import jax
import jax.numpy as jnp
import numpy as np
from jax import lax
from jax.experimental import pallas as pl
from jax.experimental.pallas import tpu as pltpu
from jax.sharding import PartitionSpec as P

CELL_X = 8
CELL_Y = 128
CELL_Z = 16
CHANNELS = 64
COMPS = 3
HALO = 4
ROW = CELL_Y + 2 * HALO
NT = (((1,), (1,)), ((), ()))


def twiddle_table(count):
    position = jnp.arange(count, dtype=jnp.int32)
    phase = position[:, None] * position[None, :] % count
    angle = phase.astype(jnp.float32) * (2.0 * math.pi / count)
    factor = 1.0 / math.sqrt(count)
    return jnp.stack([jnp.cos(angle) * factor, -jnp.sin(angle) * factor]).astype(jnp.bfloat16)


def three_parts(value):
    high = value.astype(jnp.bfloat16).astype(jnp.float32)
    rest = value - high
    middle = rest.astype(jnp.bfloat16).astype(jnp.float32)
    return high, middle, rest - middle


def pack(dest_ref, cell_ref, value_ref, out_ref):
    bricks, _, slots = out_ref.shape
    rows = dest_ref.shape[1]
    block = min(256, rows)
    upper = (
        lax.broadcasted_iota(jnp.int32, (block, block), 0)
        < lax.broadcasted_iota(jnp.int32, (block, block), 1)
    ).astype(jnp.float32).astype(jnp.bfloat16)
    brick_ids = lax.broadcasted_iota(jnp.int32, (bricks, block), 0)
    slot_ids = lax.broadcasted_iota(jnp.int32, (slots, block), 0)
    start = jnp.zeros((bricks, 1), jnp.float32)
    total = jnp.zeros((12 * bricks, slots), jnp.float32)
    for number in range(rows // block):
        span = slice(number * block, (number + 1) * block)
        hot = (brick_ids == dest_ref[:, span]).astype(jnp.float32)
        before = jnp.dot(hot.astype(jnp.bfloat16), upper, preferred_element_type=jnp.float32)
        slot = jnp.sum(hot * (before + start), axis=0, keepdims=True).astype(jnp.int32)
        start = start + jnp.sum(hot, axis=1, keepdims=True)
        slot_hot = (slot_ids == slot).astype(jnp.float32).astype(jnp.bfloat16)
        data = [cell_ref[:, span].astype(jnp.float32)]
        data += [value_ref[f : f + 1, span] for f in range(COMPS)]
        spread = [hot * part for row in data for part in three_parts(row)]
        total = total + lax.dot_general(
            jnp.concatenate(spread, axis=0).astype(jnp.bfloat16),
            slot_hot,
            NT,
            preferred_element_type=jnp.float32,
        )
    for w in range(COMPS + 1):
        parts = [total[(3 * w + i) * bricks : (3 * w + i + 1) * bricks] for i in range(3)]
        out_ref[:, w, :] = (parts[0] + parts[1]) + parts[2]


def paint(in_ref, cells_ref, edge_ref):
    bricks, _, slots = in_ref.shape
    group = max(1, 512 // slots)
    block = group * slots
    lines = CELL_Z * CELL_X
    high_ids = lax.broadcasted_iota(jnp.int32, (lines, block), 0)
    total = jnp.zeros((lines, 9 * CELL_Y), jnp.float32)
    for first in range(0, bricks, group):
        rows = jnp.concatenate([in_ref[first + i] for i in range(group)], axis=1)
        cell = rows[:1].astype(jnp.int32)
        line = cell // CELL_Y
        line = line % CELL_X * CELL_Z + line // CELL_X
        high_hot = (high_ids == line).astype(jnp.float32).astype(jnp.bfloat16)
        low_hot = (high_ids == cell % CELL_Y).astype(jnp.float32)
        spread = []
        for f in range(COMPS):
            for part in three_parts(rows[f + 1 : f + 2]):
                spread.append((low_hot * part).astype(jnp.bfloat16))
        total = total + lax.dot_general(
            high_hot, jnp.concatenate(spread, axis=0), NT, preferred_element_type=jnp.float32
        )
    lanes = lax.broadcasted_iota(jnp.int32, (PLANES, CELL_Y), 1)
    edge = jnp.zeros((PLANES, CELL_Y), jnp.float32)
    for x in range(CELL_X):
        fields = []
        for f in range(COMPS):
            parts = [
                total[
                    x * CELL_Z : (x + 1) * CELL_Z,
                    (3 * f + i) * CELL_Y : (3 * f + i + 1) * CELL_Y,
                ]
                for i in range(3)
            ]
            fields.append((parts[0] + parts[1]) + parts[2])
        tile = jnp.concatenate(fields, axis=0).astype(jnp.bfloat16)
        cells_ref[:, x * CELL_Y : (x + 1) * CELL_Y] = tile
        tile = tile.astype(jnp.float32)
        head = pltpu.roll(tile, 8 * x, 1) if x else tile
        tail = pltpu.roll(tile, 8 * x + 8, 1)
        edge = jnp.where((lanes >= 8 * x) & (lanes < 8 * x + 4), head, edge)
        edge = jnp.where((lanes >= 8 * x + 4) & (lanes < 8 * x + 8), tail, edge)
    edge_ref[...] = edge.astype(jnp.bfloat16)


def up(number):
    return -(-number // 128) * 128


WIDE_0 = up((CELL_X + 8) * ROW)
WIDE_1 = up((CELL_X + 6) * ROW)
WIDE_2 = up((CELL_X + 2) * ROW)
WIDE_3 = up(CELL_X * ROW)
HELD_0 = WIDE_0 + 128
HELD_1 = WIDE_1 + 128
HELD_2 = WIDE_2 + 128
TAPS_1 = 512


def chunks(width):
    return [(at, min(256, width - at)) for at in range(0, width, 256)]


def window(load, offset, size):
    first, turn = offset // 128 * 128, offset % 128
    if turn == 0:
        return load(first, size)
    return pltpu.roll(load(first, size + 128), size + 128 - turn, 1)[:, :size]


def leaky(value):
    return jnp.maximum(value, 0.1 * value)


MESH = pl.DeviceIdType.MESH
PLANES = CELL_Z * COMPS


def neighbours(count_x, count_y, me_x, me_y):
    around = []
    for dx in (-1, 0, 1):
        for dy in (-1, 0, 1):
            if dx or dy:
                place = (lax.rem(me_x + dx + count_x, count_x), lax.rem(me_y + dy + count_y, count_y))
                around.append((dx, dy, place))
    return around


def conv_kernel(
    count_x,
    count_y,
    dest_ref,
    cell_ref,
    value_ref,
    w1_ref,
    pick_any,
    w2_any,
    w3_any,
    out_ref,
    pick_ref,
    w2_ref,
    w3_ref,
    outgoing,
    incoming,
    cells_ref,
    edge_ref,
    side,
    corner,
    painted,
    big,
    mid,
    last,
    first,
    second,
    total_2,
    total_3,
    third,
    halo_send,
    halo_recv,
    plane_send,
    plane_recv,
    brick_send,
    brick_recv,
    fetched,
):
    depth = CELL_Z
    share = depth // count_x
    me_x, me_y = lax.axis_index("bx"), lax.axis_index("by")
    around = neighbours(count_x, count_y, me_x, me_y)

    devices_all = count_x * count_y
    me = me_x * count_y + me_y

    barrier = pltpu.get_barrier_semaphore()

    def greet(step, carry):
        other = lax.rem(me + step, devices_all)
        pl.semaphore_signal(
            barrier,
            inc=1,
            device_id=(other // count_y, lax.rem(other, count_y)),
            device_id_type=MESH,
        )
        return carry

    lax.fori_loop(1, devices_all, greet, 0)
    fetches = []
    for number, (source, target) in enumerate(
        ((pick_any, pick_ref), (w2_any, w2_ref), (w3_any, w3_ref))
    ):
        fetch = pltpu.make_async_copy(source, target, fetched.at[number])
        fetch.start()
        fetches.append(fetch)
    pack(dest_ref, cell_ref, value_ref, outgoing)
    pl.semaphore_wait(barrier, devices_all - 1)

    def brick_copy(slot, other):
        return pltpu.make_async_remote_copy(
            src_ref=outgoing.at[other],
            dst_ref=incoming.at[slot],
            send_sem=brick_send.at[other],
            recv_sem=brick_recv.at[slot],
            device_id=(other // count_y, lax.rem(other, count_y)),
            device_id_type=MESH,
        )

    def send_brick(step, carry):
        brick_copy(me, lax.rem(me + step, devices_all)).start()
        return carry

    lax.fori_loop(1, devices_all, send_brick, 0)
    incoming[me] = outgoing[me]
    for fetch in fetches:
        fetch.wait()

    def spread_weight(z, carry):
        rows = pl.ds(pl.multiple_of(z * CHANNELS, CHANNELS), CHANNELS)
        big[rows, :] = jnp.dot(
            w1_ref[...], pick_ref[z], preferred_element_type=jnp.float32
        ).astype(jnp.bfloat16)
        return carry

    lax.fori_loop(0, depth, spread_weight, 0)
    for source, target in ((w2_ref, mid), (w3_ref, last)):
        for tz in range(3):
            blocks = [
                source[tap // 3, tap % 3][:, tz * CHANNELS : (tz + 1) * CHANNELS]
                for tap in range(9)
            ]
            target[tz * CHANNELS : (tz + 1) * CHANNELS, :] = jnp.concatenate(blocks, axis=1)

    def clear(z, carry):
        total_2[z] = jnp.zeros((CHANNELS, WIDE_2), jnp.float32)
        total_3[z] = jnp.zeros((CHANNELS, WIDE_3), jnp.float32)
        first[z, :, WIDE_1:] = jnp.zeros((CHANNELS, HELD_1 - WIDE_1), jnp.bfloat16)
        second[z, :, WIDE_2:] = jnp.zeros((CHANNELS, HELD_2 - WIDE_2), jnp.bfloat16)
        return carry

    lax.fori_loop(0, depth, clear, 0)
    def settle_brick(step, carry):
        other = lax.rem(me + step, devices_all)
        brick_copy(me, other).wait_send()
        brick_copy(other, other).wait_recv()
        return carry

    lax.fori_loop(1, devices_all, settle_brick, 0)
    paint(incoming, cells_ref, edge_ref)

    halo = []
    for number, (dx, dy, place) in enumerate(around):
        if dy:
            slot = (1 - dx) * 2 + (0 if dy == 1 else 1)
            source, target = edge_ref, corner.at[slot]
        elif dx == 1:
            source, target = cells_ref.at[:, HALO * CELL_Y :], side.at[0]
        else:
            source, target = cells_ref.at[:, : HALO * CELL_Y], side.at[1]
        copy = pltpu.make_async_remote_copy(
            src_ref=source,
            dst_ref=target,
            send_sem=halo_send.at[number],
            recv_sem=halo_recv.at[number],
            device_id=place,
            device_id_type=MESH,
        )
        copy.start()
        halo.append(copy)

    for copy in halo:
        copy.wait()

    lanes = lax.broadcasted_iota(jnp.int32, (PLANES, CELL_Y), 1)
    before = None
    for row in range(CELL_X + 2 * HALO):
        if row < HALO:
            centre, x, group = side[0, :, row * CELL_Y : (row + 1) * CELL_Y], row + HALO, 0
        elif row < HALO + CELL_X:
            x, group = row - HALO, 1
            centre = cells_ref[:, x * CELL_Y : (x + 1) * CELL_Y]
        else:
            x, group = row - HALO - CELL_X, 2
            centre = side[1, :, x * CELL_Y : (x + 1) * CELL_Y]
        under = pltpu.roll(corner[2 * group].astype(jnp.float32), 120 - 8 * x, 1)
        over = corner[2 * group + 1].astype(jnp.float32)
        if x:
            over = pltpu.roll(over, CELL_Y - 8 * x, 1)
        joined = jnp.concatenate(
            [centre.astype(jnp.float32), jnp.where(lanes < 64, over, under)], axis=1
        )
        joined = pltpu.roll(joined, 8 * row + HALO, 1)
        tile = joined[:, :CELL_Y]
        if row:
            tile = jnp.where(lanes < 8 * row, before, tile)
        painted[:, row * CELL_Y : (row + 1) * CELL_Y] = tile.astype(jnp.bfloat16)
        before = joined[:, CELL_Y:]
    painted[:, 16 * CELL_Y : 17 * CELL_Y] = before.astype(jnp.bfloat16)
    painted[:, WIDE_0:] = jnp.zeros((PLANES, HELD_0 - WIDE_0), jnp.bfloat16)

    for at, size in chunks(WIDE_1):
        pieces = [
            window(lambda a, n: painted[:, a : a + n], at + tx * ROW + ty, size)
            for tx in range(3)
            for ty in range(3)
        ]
        pieces.append(jnp.zeros((TAPS_1 - 9 * PLANES, size), jnp.bfloat16))
        taps = jnp.concatenate(pieces, axis=0)
        for g in range(depth // 4):
            rows = slice(g * 4 * CHANNELS, (g + 1) * 4 * CHANNELS)
            value = leaky(jnp.dot(big[rows, :], taps, preferred_element_type=jnp.float32))
            value = value.astype(jnp.bfloat16)
            for i in range(4):
                first[g * 4 + i, :, at : at + size] = value[i * CHANNELS : (i + 1) * CHANNELS]

    def add_plane(source, weight_ref, total, spacing, width, z):
        for at, size in chunks(width):
            taps = jnp.concatenate(
                [
                    window(
                        lambda a, n: source[z, :, a : a + n],
                        at + (tx * ROW + ty) * spacing,
                        size,
                    )
                    for tx in range(3)
                    for ty in range(3)
                ],
                axis=0,
            )
            value = jnp.dot(weight_ref[...], taps, preferred_element_type=jnp.float32)
            places = [lax.rem(z - (tz - 1) * spacing + depth, depth) for tz in range(3)]
            sums = [
                total[to, :, at : at + size] + value[tz * CHANNELS : (tz + 1) * CHANNELS]
                for tz, to in enumerate(places)
            ]
            for to, summed in zip(places, sums):
                total[to, :, at : at + size] = summed

    def plane_copy(z):
        owner = z // share
        return pltpu.make_async_remote_copy(
            src_ref=third.at[z],
            dst_ref=out_ref.at[lax.rem(z, share), pl.ds(me_x * CELL_X, CELL_X)],
            send_sem=plane_send.at[z],
            recv_sem=plane_recv.at[me_x * share + lax.rem(z, share)],
            device_id=(owner, me_y),
            device_id_type=MESH,
        )

    begin = (me_x + 1) * share - 3 + depth

    def turn(step, carry):
        @pl.when(step < depth)
        def _():
            add_plane(first, mid, total_2, 2, WIDE_2, lax.rem(begin + step, depth))

        @pl.when((step >= 4) & (step < depth + 4))
        def _():
            z = lax.rem(begin + step - 2, depth)
            second[z, :, :WIDE_2] = leaky(total_2[z]).astype(jnp.bfloat16)
            add_plane(second, last, total_3, 1, WIDE_3, z)

        @pl.when(step >= 6)
        def _():
            z = lax.rem(begin + step - 3, depth)
            value = leaky(total_3[z])
            for x in range(CELL_X):
                third[z, x] = value[:, x * ROW : x * ROW + CELL_Y].astype(jnp.bfloat16)

            @pl.when(z // share == me_x)
            def _():
                out_ref[lax.rem(z, share), pl.ds(me_x * CELL_X, CELL_X)] = third[z]

            @pl.when(z // share != me_x)
            def _():
                plane_copy(z).start()

        return carry

    lax.fori_loop(0, depth + 6, turn, 0)

    def settle(number, carry):
        other = number // share

        @pl.when(other != me_x)
        def _():
            plane_copy(number).wait_send()
            inner = lax.rem(number, share)
            pltpu.make_async_remote_copy(
                src_ref=third.at[number],
                dst_ref=out_ref.at[inner, pl.ds(other * CELL_X, CELL_X)],
                send_sem=plane_send.at[number],
                recv_sem=plane_recv.at[number],
                device_id=(other, me_y),
                device_id_type=MESH,
            ).wait_recv()

        return carry

    lax.fori_loop(0, depth, settle, 0)


def pick_table():
    table = np.zeros((CELL_Z, 9, 3, COMPS, TAPS_1), np.float32)
    for z in range(CELL_Z):
        for tap in range(9):
            for tz in range(3):
                for i in range(COMPS):
                    plane = (z + tz - 1) % CELL_Z
                    table[z, tap, tz, i, tap * PLANES + i * CELL_Z + plane] = 1
    return table.reshape(CELL_Z, 27 * COMPS, TAPS_1)


def on_device(particle_values, destination, cell_index, weight_in, weight_mid, weight_out):
    count_x, count_y = lax.axis_size("bx"), lax.axis_size("by")
    devices_all = count_x * count_y
    share = CELL_Z // count_x
    rows_here = cell_index.shape[0]
    slots = max(128, 2 * rows_here // devices_all)
    pick = jnp.asarray(pick_table(), jnp.bfloat16)
    w1 = jnp.transpose(weight_in, (2, 0, 1, 3)).reshape(CHANNELS, 27 * COMPS)
    half = jnp.bfloat16
    moved = pl.pallas_call(
        functools.partial(conv_kernel, count_x, count_y),
        out_shape=jax.ShapeDtypeStruct((share, count_x * CELL_X, CHANNELS, CELL_Y), half),
        in_specs=[pl.BlockSpec(memory_space=pltpu.VMEM)] * 4
        + [pl.BlockSpec(memory_space=pl.ANY)] * 3,
        out_specs=pl.BlockSpec(memory_space=pltpu.VMEM),
        scratch_shapes=[
            pltpu.VMEM(pick.shape, half),
            pltpu.VMEM(weight_mid.shape, half),
            pltpu.VMEM(weight_out.shape, half),
            pltpu.VMEM((devices_all, COMPS + 1, slots), jnp.float32),
            pltpu.VMEM((devices_all, COMPS + 1, slots), jnp.float32),
            pltpu.VMEM((PLANES, CELL_X * CELL_Y), half),
            pltpu.VMEM((PLANES, CELL_Y), half),
            pltpu.VMEM((2, PLANES, HALO * CELL_Y), half),
            pltpu.VMEM((6, PLANES, CELL_Y), half),
            pltpu.VMEM((PLANES, HELD_0), half),
            pltpu.VMEM((CELL_Z * CHANNELS, TAPS_1), half),
            pltpu.VMEM((3 * CHANNELS, 9 * CHANNELS), half),
            pltpu.VMEM((3 * CHANNELS, 9 * CHANNELS), half),
            pltpu.VMEM((CELL_Z, CHANNELS, HELD_1), half),
            pltpu.VMEM((CELL_Z, CHANNELS, HELD_2), half),
            pltpu.VMEM((CELL_Z, CHANNELS, WIDE_2), jnp.float32),
            pltpu.VMEM((CELL_Z, CHANNELS, WIDE_3), jnp.float32),
            pltpu.VMEM((CELL_Z, CELL_X, CHANNELS, CELL_Y), half),
            pltpu.SemaphoreType.DMA((8,)),
            pltpu.SemaphoreType.DMA((8,)),
            pltpu.SemaphoreType.DMA((CELL_Z,)),
            pltpu.SemaphoreType.DMA((CELL_Z,)),
            pltpu.SemaphoreType.DMA((devices_all,)),
            pltpu.SemaphoreType.DMA((devices_all,)),
            pltpu.SemaphoreType.DMA((3,)),
        ],
        compiler_params=pltpu.CompilerParams(
            vmem_limit_bytes=48 * 2**20, collective_id=0, has_side_effects=True
        ),
        name="fields",
    )(
        destination.reshape(1, rows_here),
        cell_index.reshape(1, rows_here),
        particle_values,
        w1,
        pick,
        weight_mid,
        weight_out,
    )
    twiddle = twiddle_table(moved.shape[1])
    return jnp.einsum(
        "tkx,zxcy->tczky", twiddle, moved, preferred_element_type=jnp.float32
    ).astype(jnp.bfloat16)


def solution(mesh):
    placed = (P(None, ("bx", "by")), P(("bx", "by"), None), P(("bx", "by")), P(), P(), P())
    return jax.shard_map(
        on_device,
        mesh=mesh,
        in_specs=placed,
        out_specs=P(None, None, "bx", None, "by"),
        check_vma=False,
    )
```
